32 devices in a mesh: grp: 4 (over y, core), shard: 8 (over z, x).
Axes of the slice: x: 2, y: 2, z: 4, core: 2. Of those that a mesh axis runs over, the one named last changes fastest.
Arguments:
- regressors: bfloat16 [98304, 512], P(('grp', 'shard')), may hold values from -40 to 40
- targets: bfloat16 [98304, 512], P(('grp', 'shard')), may hold values from -120 to 120
Outputs:
- predictor: float32 [512, 512], replicated
- residuals: bfloat16 [98304, 512], P(('grp', 'shard'))
The draws below stay inside these ranges and needn't reach their ends.
All inputs are finite; a program needn't handle non-finite values.
Results may differ from the reference program's by a relative error of at most 0.0013.
Values sent between devices are 32-bit elements; how exact they have to be, the bound alone decides.
A program may use at most 64 MiB of HBM per device.

```python
import math
import jax
import jax.numpy as jnp
from jax import lax

K = 512
P_SIZE = 512
ROWS_DEV = 3072
ROWS = 98304
N_GRP = 4
N_SHARD = 8


def telemetry(key):
    times = jnp.arange(ROWS, dtype=jnp.float32) / ROWS
    trend = jnp.exp(math.log(3.0) * times)
    mixing = 0.8
    factor_row = jnp.exp(jax.random.uniform(jax.random.fold_in(key, 11), (ROWS,), jnp.float32, math.log(0.5), math.log(2.0)))
    fresh = jnp.clip(jax.random.normal(jax.random.fold_in(key, 12), (ROWS, K), jnp.float32), -4.5, 4.5)
    base = (fresh + mixing * jnp.roll(fresh, 1, axis=1)) / math.sqrt(1.0 + mixing * mixing)
    amplitude = trend * factor_row
    modes = base * amplitude[:, None]
    coeff_mean = jax.random.uniform(jax.random.fold_in(key, 21), (P_SIZE,), jnp.float32, -1.0, 1.0)
    coeff_swing = jax.random.uniform(jax.random.fold_in(key, 22), (P_SIZE,), jnp.float32, 0.3, 0.8)
    phases = jax.random.uniform(jax.random.fold_in(key, 23), (P_SIZE,), jnp.float32, 0.0, 1.0)
    coupling = jax.random.uniform(jax.random.fold_in(key, 24), (P_SIZE,), jnp.float32, -0.5, 0.5)
    coeff_now = coeff_mean[None, :] + coeff_swing[None, :] * jnp.sin(2.0 * math.pi * (phases[None, :] + 3.0 * times[:, None]))
    neighbour = jnp.roll(modes, -1, axis=1)[:, :P_SIZE]
    noise_part = 0.5 * jnp.clip(jax.random.normal(jax.random.fold_in(key, 25), (ROWS, P_SIZE), jnp.float32), -4.5, 4.5) * amplitude[:, None]
    future = coeff_now * modes[:, :P_SIZE] + coupling[None, :] * neighbour + noise_part
    return (modes, future)


def draw_regressors(key, part):
    return telemetry(key)[0].astype(jnp.bfloat16)


def draw_targets(key, part):
    return telemetry(key)[1].astype(jnp.bfloat16)


def setup_inputs(seed: int = 0) -> dict:
    seeds = jax.random.split(jax.random.key(seed), 3)
    return {
        "regressors": draw_regressors(jax.random.fold_in(seeds[2], 71), 0),
        "targets": draw_targets(jax.random.fold_in(seeds[2], 71), 0),
    }


def solve_predictor(factor, cross_sum):
    interim = jax.scipy.linalg.solve_triangular(factor, cross_sum, lower=True)
    return jax.scipy.linalg.solve_triangular(factor, interim, lower=True, trans=1)

def residual_block(rows_x, rows_y, predictor):
    pred_high = predictor.astype(jnp.bfloat16)
    pred_low = (predictor - lax.optimization_barrier(pred_high).astype(jnp.float32)).astype(jnp.bfloat16)
    estimate = jnp.dot(rows_x.astype(jnp.float32), pred_high.astype(jnp.float32), preferred_element_type=jnp.float32) + jnp.dot(rows_x.astype(jnp.float32), pred_low.astype(jnp.float32), preferred_element_type=jnp.float32)
    return (rows_y.astype(jnp.float32) - estimate).astype(jnp.bfloat16)

def reference(regressors, targets):
    gram_total = jnp.dot(regressors.T.astype(jnp.float32), regressors.astype(jnp.float32), preferred_element_type=jnp.float32)
    cross_total = jnp.dot(regressors.T.astype(jnp.float32), targets.astype(jnp.float32), preferred_element_type=jnp.float32)
    factor = jnp.linalg.cholesky(gram_total)
    predictor = solve_predictor(factor, cross_total)
    blocks_x = regressors.reshape(N_GRP * N_SHARD, ROWS_DEV, K)
    blocks_y = targets.reshape(N_GRP * N_SHARD, ROWS_DEV, P_SIZE)
    residuals = lax.map(lambda pair: residual_block(pair[0], pair[1], predictor), (blocks_x, blocks_y))
    return (predictor, residuals.reshape(ROWS, P_SIZE))
```

```python
import functools

import jax
import jax.numpy as jnp
from jax import lax
from jax.experimental import pallas as pl
from jax.experimental.pallas import tpu as pltpu
from jax.sharding import PartitionSpec as P

MESH = pl.DeviceIdType.MESH
BLK = 128
GRP8 = 8
HIGHEST = lax.Precision.HIGHEST


def dot32(a, b):
    return jnp.dot(a, b, preferred_element_type=jnp.float32, precision=HIGHEST)


def phases(n_grp, n_shard):
    g, s = lax.axis_index("grp"), lax.axis_index("shard")
    cores = 2 if n_grp % 2 == 0 else 1
    ny = n_grp // cores
    nx = ny if n_shard % ny == 0 else 1
    nz = n_shard // nx
    y, core = g // cores, g % cores
    z, x = s // nx, s % nx
    core_ph = (cores, core, lambda q: (y * cores + q, s))
    plane_ph = (
        ny * nx,
        y * nx + x,
        lambda q: ((q // nx) * cores + core, z * nx + q % nx),
    )
    line_ph = (nz, z, lambda q: (g, q * nx + x))
    return core_ph, plane_ph, line_ph


def split_rows(rows, n):
    unit = 8 * n
    units = rows // unit
    first = max(1, (units * 2 + 1) // 3)
    if units < 2:
        return (rows,)
    return (first * unit, (units - first) * unit)


def part_phases(n_grp, n_shard, n_parts):
    a, b, c = phases(n_grp, n_shard)
    orders = [(a, b, c), (a, c, b)][:n_parts]
    return orders


def phase_sizes(n_grp, n_shard, n_parts):
    cores = 2 if n_grp % 2 == 0 else 1
    ny = n_grp // cores
    nx = ny if n_shard % ny == 0 else 1
    nz = n_shard // nx
    return [(cores, ny * nx, nz), (cores, nz, ny * nx)][:n_parts]


def reduce_kernel(n_grp, n_shard, parts, in_ref, out_ref, *scratch):
    n_parts = len(parts)
    recv = [scratch[3 * p : 3 * p + 3] for p in range(n_parts)]
    acc, send_sem, recv_sem, send2, recv2 = scratch[3 * n_parts :]
    orders = part_phases(n_grp, n_shard, n_parts)

    barrier = pltpu.get_barrier_semaphore()
    count = 0
    for m, me, dev in orders[0]:
        for d in range(1, m):
            pl.semaphore_signal(
                barrier, inc=1, device_id=dev((me + d) % m), device_id_type=MESH
            )
            count += 1
    pl.semaphore_wait(barrier, count)

    starts = [sum(parts[:p]) for p in range(n_parts)]
    bases = [[starts[p]] for p in range(n_parts)]
    lens = [[parts[p]] for p in range(n_parts)]

    def scatter_start(p, i):
        m, me, dev = orders[p][i]
        size = lens[p][i] // m
        src = in_ref if i == 0 else acc
        copies = []
        for d in range(1, m):
            q = (me + d) % m
            c = pltpu.make_async_remote_copy(
                src_ref=src.at[pl.ds(pl.multiple_of(bases[p][i] + q * size, 8), size)],
                dst_ref=recv[p][i].at[d - 1],
                send_sem=send_sem.at[p, i, d - 1],
                recv_sem=recv_sem.at[p, i, d - 1],
                device_id=dev(q),
                device_id_type=MESH,
            )
            c.start()
            copies.append(c)
        return copies

    def scatter_finish(p, i, copies):
        m, me, _ = orders[p][i]
        size = lens[p][i] // m
        base = pl.multiple_of(bases[p][i] + me * size, 8)
        src = in_ref if i == 0 else acc
        total = src[pl.ds(base, size)]
        for d in range(1, m):
            copies[d - 1].wait_recv()
            total = total + recv[p][i][d - 1]
        dst = out_ref if i == 2 else acc
        dst[pl.ds(base, size)] = total
        bases[p].append(base)
        lens[p].append(size)

    def gather_start(p, i):
        m, me, dev = orders[p][i]
        size = lens[p][i + 1]
        mine = out_ref.at[pl.ds(bases[p][i + 1], size)]
        copies = []
        for d in range(1, m):
            c = pltpu.make_async_remote_copy(
                src_ref=mine,
                dst_ref=mine,
                send_sem=send2.at[p, i, d - 1],
                recv_sem=recv2.at[p, i, d - 1],
                device_id=dev((me + d) % m),
                device_id_type=MESH,
            )
            c.start()
            copies.append(c)
        return copies

    sent = []
    live = [scatter_start(p, 0) for p in range(n_parts)]
    for i in range(3):
        for p in range(n_parts):
            scatter_finish(p, i, live[p])
            sent += live[p]
            live[p] = scatter_start(p, i + 1) if i < 2 else gather_start(p, 2)
    for i in (2, 1, 0):
        for p in range(n_parts):
            for c in live[p]:
                c.wait_recv()
            sent += live[p]
            live[p] = gather_start(p, i - 1) if i > 0 else []
    for c in sent:
        c.wait_send()


def all_reduce(blocks, n_grp, n_shard):
    n = n_grp * n_shard
    rows = blocks.shape[0]
    padded = -(-rows // (8 * n)) * (8 * n)
    if padded != rows:
        blocks = jnp.pad(blocks, ((0, padded - rows), (0, 0)))
    parts = split_rows(padded, n)
    sizes = phase_sizes(n_grp, n_shard, len(parts))
    most = max(max(m) for m in sizes)
    scratch = []
    for part, ms in zip(parts, sizes):
        size = part
        for m in ms:
            size //= m
            scratch.append(pltpu.VMEM((max(m - 1, 1), size, BLK), jnp.float32))
    sems = pltpu.SemaphoreType.DMA((len(parts), 3, max(most - 1, 1)))
    scratch += [pltpu.VMEM((padded, BLK), jnp.float32), sems, sems, sems, sems]
    return pl.pallas_call(
        functools.partial(reduce_kernel, n_grp, n_shard, parts),
        out_shape=jax.ShapeDtypeStruct((padded, BLK), jnp.float32),
        in_specs=[pl.BlockSpec(memory_space=pltpu.VMEM)],
        out_specs=pl.BlockSpec(memory_space=pltpu.VMEM),
        scratch_shapes=scratch,
        compiler_params=pltpu.CompilerParams(
            collective_id=0, has_side_effects=True, vmem_limit_bytes=40 * 2**20
        ),
        name="reduce_terms",
    )(blocks)


def invert_block(a):
    sub = lax.broadcasted_iota(jnp.int32, (GRP8, BLK), 0)
    lane8 = lax.broadcasted_iota(jnp.int32, (GRP8, BLK), 1)
    lane = lax.broadcasted_iota(jnp.int32, (BLK, BLK), 1)
    for g in range(BLK // GRP8):
        lo = g * GRP8
        cols = [
            jnp.broadcast_to(a[:, lo + c : lo + c + 1], (BLK, BLK)) for c in range(GRP8)
        ]
        own = [c[lo : lo + GRP8, :] for c in cols]
        inside = (lane8 >= lo) & (lane8 < lo + GRP8)
        r = jnp.where(
            inside, jnp.where(lane8 - lo == sub, 1.0, 0.0), a[lo : lo + GRP8, :]
        )
        for k in range(GRP8):
            at = sub == k
            pivot = jnp.broadcast_to(own[k][k : k + 1, :], (GRP8, BLK))
            mult = jnp.where(at, -1.0, own[k]) / pivot
            for c in range(k + 1, GRP8):
                row = jnp.broadcast_to(own[c][k : k + 1, :], (GRP8, BLK))
                own[c] = jnp.where(at, 0.0, own[c]) - mult * row
            row = jnp.broadcast_to(r[k : k + 1, :], (GRP8, BLK))
            r = jnp.where(at, 0.0, r) - mult * row
        rest = jnp.where((lane >= lo) & (lane < lo + GRP8), 0.0, a)
        for c in range(GRP8):
            rest = rest - cols[c] * jnp.broadcast_to(r[c : c + 1, :], (BLK, BLK))
        pieces = [rest[:lo]] * (lo > 0) + [r] + [rest[lo + GRP8 :]] * (lo + GRP8 < BLK)
        a = jnp.concatenate(pieces, axis=0)
    return a


def solve_kernel(
    nk, nt, tiles, b_ref, x_hbm, y_hbm, pred_ref, res_hbm,
    gram, cross, panel, high, low, xv, yv, ov, in_sem, out_sem,
):
    load_x = pltpu.make_async_copy(x_hbm, xv, in_sem.at[0])
    load_y = pltpu.make_async_copy(y_hbm, yv, in_sem.at[1])
    load_x.start()
    load_y.start()

    at = 0
    for i in range(nk):
        for j in range(i + 1):
            block = b_ref[at * BLK : (at + 1) * BLK, :]
            at += 1
            gram[i * BLK : (i + 1) * BLK, j * BLK : (j + 1) * BLK] = block
            if i != j:
                gram[j * BLK : (j + 1) * BLK, i * BLK : (i + 1) * BLK] = block.T
    for i in range(nk):
        for j in range(nt):
            cross[i * BLK : (i + 1) * BLK, j * BLK : (j + 1) * BLK] = b_ref[
                at * BLK : (at + 1) * BLK, :
            ]
            at += 1

    def stage(j, carry):
        here = pl.ds(pl.multiple_of(j * BLK, BLK), BLK)
        inverse = invert_block(gram[here, here])
        panel[...] = dot32(inverse, gram[here, :])
        panel[:, here] = inverse
        side = gram[:, here]
        gram[:, here] = jnp.zeros_like(side)
        gram[...] -= dot32(side, panel[...])
        gram[here, :] = panel[...]
        return carry

    lax.fori_loop(0, nk, stage, 0)
    pred = dot32(gram[...], cross[...])
    pred_ref[...] = pred
    top = pred.astype(jnp.bfloat16)
    high[...] = top
    low[...] = (pred - top.astype(jnp.float32)).astype(jnp.bfloat16)

    load_x.wait()
    load_y.wait()
    rows = xv.shape[0] // tiles
    stores = []
    for t in range(tiles):
        span = pl.ds(t * rows, rows)
        x = xv[span, :]
        estimate = jnp.dot(x, high[...], preferred_element_type=jnp.float32) + jnp.dot(
            x, low[...], preferred_element_type=jnp.float32
        )
        ov[span, :] = (yv[span, :].astype(jnp.float32) - estimate).astype(jnp.bfloat16)
        store = pltpu.make_async_copy(ov.at[span, :], res_hbm.at[span, :], out_sem.at[t])
        store.start()
        stores.append(store)
    for store in stores:
        store.wait()


def solve(total, regressors, targets):
    rows, k = regressors.shape
    p = targets.shape[1]
    tiles = 6 if rows % 96 == 0 else 1
    anywhere = pl.BlockSpec(memory_space=pl.ANY)
    in_vmem = pl.BlockSpec(memory_space=pltpu.VMEM)
    return pl.pallas_call(
        functools.partial(solve_kernel, k // BLK, p // BLK, tiles),
        out_shape=(
            jax.ShapeDtypeStruct((k, p), jnp.float32),
            jax.ShapeDtypeStruct((rows, p), jnp.bfloat16),
        ),
        in_specs=[in_vmem, anywhere, anywhere],
        out_specs=(in_vmem, anywhere),
        scratch_shapes=[
            pltpu.VMEM((k, k), jnp.float32),
            pltpu.VMEM((k, p), jnp.float32),
            pltpu.VMEM((BLK, k), jnp.float32),
            pltpu.VMEM((k, p), jnp.bfloat16),
            pltpu.VMEM((k, p), jnp.bfloat16),
            pltpu.VMEM((rows, k), jnp.bfloat16),
            pltpu.VMEM((rows, p), jnp.bfloat16),
            pltpu.VMEM((rows, p), jnp.bfloat16),
            pltpu.SemaphoreType.DMA((2,)),
            pltpu.SemaphoreType.DMA((tiles,)),
        ],
        compiler_params=pltpu.CompilerParams(vmem_limit_bytes=48 * 2**20),
        name="solve_and_residual",
    )(total, regressors, targets)


def body(n_grp, n_shard, regressors, targets):
    contract = (((0,), (0,)), ((), ()))
    gram = lax.dot_general(
        regressors, regressors, contract, preferred_element_type=jnp.float32
    )
    cross = lax.dot_general(
        regressors, targets, contract, preferred_element_type=jnp.float32
    )
    nk, nt = gram.shape[0] // BLK, cross.shape[1] // BLK

    def block(m, i, j):
        return m[i * BLK : (i + 1) * BLK, j * BLK : (j + 1) * BLK]

    blocks = [block(gram, i, j) for i in range(nk) for j in range(i + 1)]
    blocks += [block(cross, i, j) for i in range(nk) for j in range(nt)]
    total = all_reduce(jnp.concatenate(blocks, axis=0), n_grp, n_shard)
    return solve(total, regressors, targets)


def solution(mesh):
    placed = (P(("grp", "shard"), None), P(("grp", "shard"), None))
    return jax.shard_map(
        functools.partial(body, mesh.shape["grp"], mesh.shape["shard"]),
        mesh=mesh,
        in_specs=placed,
        out_specs=(P(), P(("grp", "shard"), None)),
        check_vma=False,
    )
```

```python
import functools

import jax
import jax.numpy as jnp
from jax import lax
from jax.experimental import pallas as pl
from jax.experimental.pallas import tpu as pltpu
from jax.sharding import PartitionSpec as P

MESH = pl.DeviceIdType.MESH
BLK = 128
GRP8 = 8
HIGHEST = lax.Precision.HIGHEST


def dot32(a, b):
    return jnp.dot(a, b, preferred_element_type=jnp.float32, precision=HIGHEST)


def phases(n_grp, n_shard):
    g, s = lax.axis_index("grp"), lax.axis_index("shard")
    cores = 2 if n_grp % 2 == 0 else 1
    ny = n_grp // cores
    nx = ny if n_shard % ny == 0 else 1
    nz = n_shard // nx
    y, core = g // cores, g % cores
    z, x = s // nx, s % nx
    core_ph = (cores, core, lambda q: (y * cores + q, s))
    plane_ph = (
        ny * nx,
        y * nx + x,
        lambda q: ((q // nx) * cores + core, z * nx + q % nx),
    )
    line_ph = (nz, z, lambda q: (g, q * nx + x))
    return core_ph, plane_ph, line_ph


def split_rows(rows, n):
    unit = 8 * n
    units = rows // unit
    if units < 2:
        return (rows,)
    first = max(1, (units * 2 + 1) // 3)
    return (first * unit, (units - first) * unit)


def phase_sizes(n_grp, n_shard, n_parts):
    cores = 2 if n_grp % 2 == 0 else 1
    ny = n_grp // cores
    nx = ny if n_shard % ny == 0 else 1
    nz = n_shard // nx
    return [(cores, ny * nx, nz), (cores, nz, ny * nx)][:n_parts]


class Sum:
    def __init__(self, src, out, parts, orders, scratch):
        self.src, self.out, self.orders = src, out, orders
        self.recv = [scratch[3 * p : 3 * p + 3] for p in range(len(parts))]
        self.acc, *self.sems = scratch[3 * len(parts) :]
        starts = [sum(parts[:p]) for p in range(len(parts))]
        self.bases, self.lens = [], []
        for start, rows, order in zip(starts, parts, orders):
            bases, lens = [start], [rows]
            for m, me, _ in order:
                lens.append(lens[-1] // m)
                bases.append(pl.multiple_of(bases[-1] + me * lens[-1], 8))
            self.bases.append(bases)
            self.lens.append(lens)
        self.n_parts = len(parts)

    def scatter(self, p, i):
        m, me, dev = self.orders[p][i]
        size = self.lens[p][i + 1]
        src = self.src if i == 0 else self.acc
        copies = []
        for d in range(1, m):
            q = (me + d) % m
            at = pl.multiple_of(self.bases[p][i] + q * size, 8)
            copies.append(
                pltpu.make_async_remote_copy(
                    src_ref=src.at[pl.ds(at, size)],
                    dst_ref=self.recv[p][i].at[d - 1],
                    send_sem=self.sems[0].at[p, i, d - 1],
                    recv_sem=self.sems[1].at[p, i, d - 1],
                    device_id=dev(q),
                    device_id_type=MESH,
                )
            )
        return copies

    def gather(self, p, i):
        m, me, dev = self.orders[p][i]
        mine = self.out.at[pl.ds(self.bases[p][i + 1], self.lens[p][i + 1])]
        return [
            pltpu.make_async_remote_copy(
                src_ref=mine,
                dst_ref=mine,
                send_sem=self.sems[2].at[p, i, d - 1],
                recv_sem=self.sems[3].at[p, i, d - 1],
                device_id=dev((me + d) % m),
                device_id_type=MESH,
            )
            for d in range(1, m)
        ]

    def add(self, p, i):
        copies = self.scatter(p, i)
        src = self.src if i == 0 else self.acc
        dst = self.out if i == 2 else self.acc
        span = pl.ds(self.bases[p][i + 1], self.lens[p][i + 1])
        total = src[span]
        for d, copy in enumerate(copies):
            copy.wait_recv()
            total = total + self.recv[p][i][d]
        dst[span] = total

    def step(self, t):
        for p in range(self.n_parts):
            if 1 <= t <= 3:
                self.add(p, t - 1)
            elif t > 3:
                for copy in self.gather(p, 6 - t):
                    copy.wait_recv()
            if t < 3:
                started = self.scatter(p, t)
            elif t < 6:
                started = self.gather(p, 5 - t)
            else:
                started = []
            for copy in started:
                copy.start()

    def finish(self):
        for p in range(self.n_parts):
            for i in range(3):
                for copy in self.scatter(p, i) + self.gather(p, i):
                    copy.wait_send()


def sum_scratch(rows, n_grp, n_shard):
    parts = split_rows(rows, n_grp * n_shard)
    sizes = phase_sizes(n_grp, n_shard, len(parts))
    most = max(max(m) for m in sizes)
    scratch = []
    for part, ms in zip(parts, sizes):
        size = part
        for m in ms:
            size //= m
            scratch.append(pltpu.VMEM((max(m - 1, 1), size, BLK), jnp.float32))
    sems = pltpu.SemaphoreType.DMA((len(parts), 3, max(most - 1, 1)))
    scratch += [pltpu.VMEM((rows, BLK), jnp.float32), sems, sems, sems, sems]
    return parts, scratch


def normal_kernel(
    n_grp, n_shard, nk, nt, g_parts, c_parts, gram_in, x_hbm, y_hbm,
    gram, cross_out, xv, yv, cross_in, gram_out, panel, in_sem, *scratch,
):
    load_x = pltpu.make_async_copy(x_hbm, xv, in_sem.at[0])
    load_y = pltpu.make_async_copy(y_hbm, yv, in_sem.at[1])
    load_x.start()
    load_y.start()

    a, b, c = phases(n_grp, n_shard)
    barrier = pltpu.get_barrier_semaphore()
    count = 0
    for m, me, dev in (a, b, c):
        for d in range(1, m):
            pl.semaphore_signal(
                barrier, inc=1, device_id=dev((me + d) % m), device_id_type=MESH
            )
            count += 1
    pl.semaphore_wait(barrier, count)

    orders = [(a, b, c), (a, c, b)]
    n_first = 3 * len(g_parts) + 5
    gsum = Sum(gram_in, gram_out, g_parts, orders[: len(g_parts)], scratch[:n_first])
    csum = Sum(cross_in, cross_out, c_parts, orders[: len(c_parts)], scratch[n_first:])

    gsum.step(0)
    gsum.step(1)
    load_x.wait()
    load_y.wait()
    used = nk * nt * BLK
    if used < cross_in.shape[0]:
        cross_in[used:, :] = jnp.zeros((cross_in.shape[0] - used, BLK), jnp.float32)
    wide = 2 if nt % 2 == 0 else 1

    def cross_columns(j):
        part = lax.dot_general(
            xv[...],
            yv[:, j * BLK : (j + wide) * BLK],
            (((0,), (0,)), ((), ())),
            preferred_element_type=jnp.float32,
        )
        for w in range(wide):
            cross_in[(j + w) * nk * BLK : (j + w + 1) * nk * BLK, :] = part[
                :, w * BLK : (w + 1) * BLK
            ]

    columns = list(range(0, nt, wide))
    for j in columns[: len(columns) // 2]:
        cross_columns(j)
    gsum.step(2)
    for j in columns[len(columns) // 2 :]:
        cross_columns(j)
    gsum.step(3)
    csum.step(0)
    for t in (4, 5, 6):
        gsum.step(t)

    at = 0
    for i in range(nk):
        for j in range(i + 1):
            block = gram_out[at * BLK : (at + 1) * BLK, :]
            at += 1
            gram[i * BLK : (i + 1) * BLK, j * BLK : (j + 1) * BLK] = block
            if i != j:
                gram[j * BLK : (j + 1) * BLK, i * BLK : (i + 1) * BLK] = block.T
    csum.step(1)

    def stage(j, carry):
        here = pl.ds(pl.multiple_of(j * BLK, BLK), BLK)
        inverse = invert_block(gram[here, here])
        for t in range(min(nk, 5)):
            @pl.when(j == t)
            def _(t=t):
                csum.step(t + 2)

        panel[...] = dot32(inverse, gram[here, :])
        panel[:, here] = inverse
        side = gram[:, here]
        gram[:, here] = jnp.zeros_like(side)
        gram[...] -= dot32(side, panel[...])
        gram[here, :] = panel[...]
        return carry

    lax.fori_loop(0, nk, stage, 0)
    for t in range(min(nk, 5) + 2, 7):
        csum.step(t)
    gsum.finish()
    csum.finish()


def normal_equations(blocks, regressors, targets, n_grp, n_shard):
    rows, k = regressors.shape
    p = targets.shape[1]
    nk, nt = k // BLK, p // BLK
    unit = 8 * n_grp * n_shard
    padded = -(-blocks.shape[0] // unit) * unit
    if padded != blocks.shape[0]:
        blocks = jnp.pad(blocks, ((0, padded - blocks.shape[0]), (0, 0)))
    cross_rows = -(-(nk * nt * BLK) // unit) * unit
    g_parts, g_scratch = sum_scratch(padded, n_grp, n_shard)
    c_parts, c_scratch = sum_scratch(cross_rows, n_grp, n_shard)
    anywhere = pl.BlockSpec(memory_space=pl.ANY)
    in_vmem = pl.BlockSpec(memory_space=pltpu.VMEM)
    return pl.pallas_call(
        functools.partial(normal_kernel, n_grp, n_shard, nk, nt, g_parts, c_parts),
        out_shape=(
            jax.ShapeDtypeStruct((k, k), jnp.float32),
            jax.ShapeDtypeStruct((cross_rows, BLK), jnp.float32),
        ),
        in_specs=[in_vmem, anywhere, anywhere],
        out_specs=(in_vmem, in_vmem),
        scratch_shapes=[
            pltpu.VMEM((rows, k), jnp.bfloat16),
            pltpu.VMEM((rows, p), jnp.bfloat16),
            pltpu.VMEM((cross_rows, BLK), jnp.float32),
            pltpu.VMEM((padded, BLK), jnp.float32),
            pltpu.VMEM((BLK, k), jnp.float32),
            pltpu.SemaphoreType.DMA((2,)),
            *g_scratch,
            *c_scratch,
        ],
        compiler_params=pltpu.CompilerParams(
            collective_id=0, has_side_effects=True, vmem_limit_bytes=44 * 2**20
        ),
        name="normal_equations",
    )(blocks, regressors, targets)


def reciprocal(p):
    r = pl.reciprocal(p, approx=True)
    r = r * (2.0 - p * r)
    return r * (2.0 - p * r)


def invert_block(a):
    sub = lax.broadcasted_iota(jnp.int32, (GRP8, BLK), 0)
    lane8 = lax.broadcasted_iota(jnp.int32, (GRP8, BLK), 1)
    lane = lax.broadcasted_iota(jnp.int32, (BLK, BLK), 1)
    for g in range(BLK // GRP8):
        lo = g * GRP8
        cols = [
            jnp.broadcast_to(a[:, lo + c : lo + c + 1], (BLK, BLK)) for c in range(GRP8)
        ]
        own = [c[lo : lo + GRP8, :] for c in cols]
        inside = (lane8 >= lo) & (lane8 < lo + GRP8)
        r = jnp.where(
            inside, jnp.where(lane8 - lo == sub, 1.0, 0.0), a[lo : lo + GRP8, :]
        )
        for k in range(GRP8):
            at = sub == k
            pivot = jnp.broadcast_to(own[k][k : k + 1, :], (GRP8, BLK))
            mult = jnp.where(at, -1.0, own[k]) * reciprocal(pivot)
            for c in range(k + 1, GRP8):
                row = jnp.broadcast_to(own[c][k : k + 1, :], (GRP8, BLK))
                own[c] = jnp.where(at, 0.0, own[c]) - mult * row
            row = jnp.broadcast_to(r[k : k + 1, :], (GRP8, BLK))
            r = jnp.where(at, 0.0, r) - mult * row
        rest = jnp.where((lane >= lo) & (lane < lo + GRP8), 0.0, a)
        for c in range(GRP8):
            rest = rest - cols[c] * jnp.broadcast_to(r[c : c + 1, :], (BLK, BLK))
        pieces = [rest[:lo]] * (lo > 0) + [r] + [rest[lo + GRP8 :]] * (lo + GRP8 < BLK)
        a = jnp.concatenate(pieces, axis=0)
    return a


def solve_kernel(
    nk, nt, tiles, inv_ref, b_ref, x_hbm, y_hbm, pred_ref, res_hbm,
    cross, high, low, xv, yv, ov, in_sem, out_sem,
):
    load_x = pltpu.make_async_copy(x_hbm, xv, in_sem.at[0])
    load_y = pltpu.make_async_copy(y_hbm, yv, in_sem.at[1])
    load_x.start()
    load_y.start()

    depth = nk * BLK
    for j in range(nt):
        cross[:, j * BLK : (j + 1) * BLK] = b_ref[j * depth : (j + 1) * depth, :]
    pred = dot32(inv_ref[...], cross[...])
    pred_ref[...] = pred
    top = pred.astype(jnp.bfloat16)
    high[...] = top
    low[...] = (pred - top.astype(jnp.float32)).astype(jnp.bfloat16)

    load_x.wait()
    load_y.wait()
    rows = xv.shape[0] // tiles
    stores = []
    for t in range(tiles):
        span = pl.ds(t * rows, rows)
        x = xv[span, :]
        estimate = jnp.dot(x, high[...], preferred_element_type=jnp.float32) + jnp.dot(
            x, low[...], preferred_element_type=jnp.float32
        )
        ov[span, :] = (yv[span, :].astype(jnp.float32) - estimate).astype(jnp.bfloat16)
        store = pltpu.make_async_copy(ov.at[span, :], res_hbm.at[span, :], out_sem.at[t])
        store.start()
        stores.append(store)
    for store in stores:
        store.wait()


def solve(inverse, total, regressors, targets):
    rows, k = regressors.shape
    p = targets.shape[1]
    tiles = 6 if rows % 96 == 0 else 1
    anywhere = pl.BlockSpec(memory_space=pl.ANY)
    in_vmem = pl.BlockSpec(memory_space=pltpu.VMEM)
    return pl.pallas_call(
        functools.partial(solve_kernel, k // BLK, p // BLK, tiles),
        out_shape=(
            jax.ShapeDtypeStruct((k, p), jnp.float32),
            jax.ShapeDtypeStruct((rows, p), jnp.bfloat16),
        ),
        in_specs=[in_vmem, in_vmem, anywhere, anywhere],
        out_specs=(in_vmem, anywhere),
        scratch_shapes=[
            pltpu.VMEM((k, p), jnp.float32),
            pltpu.VMEM((k, p), jnp.bfloat16),
            pltpu.VMEM((k, p), jnp.bfloat16),
            pltpu.VMEM((rows, k), jnp.bfloat16),
            pltpu.VMEM((rows, p), jnp.bfloat16),
            pltpu.VMEM((rows, p), jnp.bfloat16),
            pltpu.SemaphoreType.DMA((2,)),
            pltpu.SemaphoreType.DMA((tiles,)),
        ],
        compiler_params=pltpu.CompilerParams(vmem_limit_bytes=48 * 2**20),
        name="solve_and_residual",
    )(inverse, total, regressors, targets)


def body(n_grp, n_shard, regressors, targets):
    contract = (((0,), (0,)), ((), ()))
    gram = lax.dot_general(
        regressors, regressors, contract, preferred_element_type=jnp.float32
    )
    nk = gram.shape[0] // BLK

    def block(i, j):
        return gram[i * BLK : (i + 1) * BLK, j * BLK : (j + 1) * BLK]

    blocks = jnp.concatenate(
        [block(i, j) for i in range(nk) for j in range(i + 1)], axis=0
    )
    inverse, total = normal_equations(blocks, regressors, targets, n_grp, n_shard)
    return solve(inverse, total, regressors, targets)


def solution(mesh):
    placed = (P(("grp", "shard"), None), P(("grp", "shard"), None))
    return jax.shard_map(
        functools.partial(body, mesh.shape["grp"], mesh.shape["shard"]),
        mesh=mesh,
        in_specs=placed,
        out_specs=(P(), P(("grp", "shard"), None)),
        check_vma=False,
    )
```

```python
import functools

import jax
import jax.numpy as jnp
from jax import lax
from jax.experimental import pallas as pl
from jax.experimental.pallas import tpu as pltpu
from jax.sharding import PartitionSpec as P

MESH = pl.DeviceIdType.MESH
BLK = 128
GRP8 = 8
HIGHEST = lax.Precision.HIGHEST


def dot32(a, b):
    return jnp.dot(a, b, preferred_element_type=jnp.float32, precision=HIGHEST)


def phases(n_grp, n_shard):
    g, s = lax.axis_index("grp"), lax.axis_index("shard")
    cores = 2 if n_grp % 2 == 0 else 1
    ny = n_grp // cores
    nx = ny if n_shard % ny == 0 else 1
    nz = n_shard // nx
    y, core = g // cores, g % cores
    z, x = s // nx, s % nx
    core_ph = (cores, core, lambda q: (y * cores + q, s))
    plane_ph = (
        ny * nx,
        y * nx + x,
        lambda q: ((q // nx) * cores + core, z * nx + q % nx),
    )
    line_ph = (nz, z, lambda q: (g, q * nx + x))
    return core_ph, plane_ph, line_ph


def split_rows(rows, n):
    unit = 8 * n
    units = rows // unit
    if units < 2:
        return (rows,)
    first = max(1, (units * 2 + 1) // 3)
    return (first * unit, (units - first) * unit)


def phase_sizes(n_grp, n_shard, n_parts):
    cores = 2 if n_grp % 2 == 0 else 1
    ny = n_grp // cores
    nx = ny if n_shard % ny == 0 else 1
    nz = n_shard // nx
    return [(cores, ny * nx, nz), (cores, nz, ny * nx)][:n_parts]


class Sum:
    def __init__(self, src, out, parts, orders, scratch):
        self.src, self.out, self.orders = src, out, orders
        self.recv = [scratch[3 * p : 3 * p + 3] for p in range(len(parts))]
        self.acc, *self.sems = scratch[3 * len(parts) :]
        starts = [sum(parts[:p]) for p in range(len(parts))]
        self.bases, self.lens = [], []
        for start, rows, order in zip(starts, parts, orders):
            bases, lens = [start], [rows]
            for m, me, _ in order:
                lens.append(lens[-1] // m)
                bases.append(pl.multiple_of(bases[-1] + me * lens[-1], 8))
            self.bases.append(bases)
            self.lens.append(lens)
        self.n_parts = len(parts)

    def scatter(self, p, i):
        m, me, dev = self.orders[p][i]
        size = self.lens[p][i + 1]
        src = self.src if i == 0 else self.acc
        copies = []
        for d in range(1, m):
            q = (me + d) % m
            at = pl.multiple_of(self.bases[p][i] + q * size, 8)
            copies.append(
                pltpu.make_async_remote_copy(
                    src_ref=src.at[pl.ds(at, size)],
                    dst_ref=self.recv[p][i].at[d - 1],
                    send_sem=self.sems[0].at[p, i, d - 1],
                    recv_sem=self.sems[1].at[p, i, d - 1],
                    device_id=dev(q),
                    device_id_type=MESH,
                )
            )
        return copies

    def gather(self, p, i):
        m, me, dev = self.orders[p][i]
        mine = self.out.at[pl.ds(self.bases[p][i + 1], self.lens[p][i + 1])]
        return [
            pltpu.make_async_remote_copy(
                src_ref=mine,
                dst_ref=mine,
                send_sem=self.sems[2].at[p, i, d - 1],
                recv_sem=self.sems[3].at[p, i, d - 1],
                device_id=dev((me + d) % m),
                device_id_type=MESH,
            )
            for d in range(1, m)
        ]

    def add(self, p, i):
        copies = self.scatter(p, i)
        src = self.src if i == 0 else self.acc
        dst = self.out if i == 2 else self.acc
        span = pl.ds(self.bases[p][i + 1], self.lens[p][i + 1])
        total = src[span]
        for d, copy in enumerate(copies):
            copy.wait_recv()
            total = total + self.recv[p][i][d]
        dst[span] = total

    def step(self, t):
        for p in range(self.n_parts):
            if 1 <= t <= 3:
                self.add(p, t - 1)
            elif t > 3:
                for copy in self.gather(p, 6 - t):
                    copy.wait_recv()
            if t < 3:
                started = self.scatter(p, t)
            elif t < 6:
                started = self.gather(p, 5 - t)
            else:
                started = []
            for copy in started:
                copy.start()

    def finish(self):
        for p in range(self.n_parts):
            for i in range(3):
                for copy in self.scatter(p, i) + self.gather(p, i):
                    copy.wait_send()


def sum_scratch(rows, n_grp, n_shard):
    parts = split_rows(rows, n_grp * n_shard)
    sizes = phase_sizes(n_grp, n_shard, len(parts))
    most = max(max(m) for m in sizes)
    scratch = []
    for part, ms in zip(parts, sizes):
        size = part
        for m in ms:
            size //= m
            scratch.append(pltpu.VMEM((max(m - 1, 1), size, BLK), jnp.float32))
    sems = pltpu.SemaphoreType.DMA((len(parts), 3, max(most - 1, 1)))
    scratch += [pltpu.VMEM((rows, BLK), jnp.float32), sems, sems, sems, sems]
    return parts, scratch


def normal_kernel(
    n_grp, n_shard, nk, g_parts, c_parts, gram_in, cross_in,
    gram, cross_out, gram_out, panel, *scratch,
):
    a, b, c = phases(n_grp, n_shard)
    barrier = pltpu.get_barrier_semaphore()
    count = 0
    for m, me, dev in (a, b, c):
        for d in range(1, m):
            pl.semaphore_signal(
                barrier, inc=1, device_id=dev((me + d) % m), device_id_type=MESH
            )
            count += 1
    pl.semaphore_wait(barrier, count)

    orders = [(a, b, c), (a, c, b)]
    n_first = 3 * len(g_parts) + 5
    gsum = Sum(gram_in, gram_out, g_parts, orders[: len(g_parts)], scratch[:n_first])
    csum = Sum(cross_in, cross_out, c_parts, orders[: len(c_parts)], scratch[n_first:])

    gsum.step(0)
    gsum.step(1)
    gsum.step(2)
    gsum.step(3)
    csum.step(0)
    for t in (4, 5, 6):
        gsum.step(t)

    eye = lax.broadcasted_iota(jnp.int32, (BLK, BLK), 0) == lax.broadcasted_iota(
        jnp.int32, (BLK, BLK), 1
    )
    down, across = [], []
    for i in range(nk):
        at = i * (i + 1) // 2 + i
        diagonal = jnp.where(eye, gram_out[at * BLK : (at + 1) * BLK, :], 0.0)
        down.append(lax.rsqrt(jnp.sum(diagonal, axis=1, keepdims=True)))
        across.append(lax.rsqrt(jnp.sum(diagonal, axis=0, keepdims=True)))
    for i in range(nk):
        for j in range(i + 1):
            at = i * (i + 1) // 2 + j
            block = gram_out[at * BLK : (at + 1) * BLK, :] * down[i] * across[j]
            gram[i * BLK : (i + 1) * BLK, j * BLK : (j + 1) * BLK] = block
            if i != j:
                gram[j * BLK : (j + 1) * BLK, i * BLK : (i + 1) * BLK] = block.T
    csum.step(1)

    def stage(j, carry):
        here = pl.ds(pl.multiple_of(j * BLK, BLK), BLK)
        inverse = invert_block(gram[here, here])
        for t in range(min(nk, 5)):
            @pl.when(j == t)
            def _(t=t):
                csum.step(t + 2)

        panel[...] = dot32(inverse, gram[here, :])
        panel[:, here] = inverse
        side = gram[:, here]
        gram[:, here] = jnp.zeros_like(side)
        gram[...] -= dot32(side, panel[...])
        gram[here, :] = panel[...]
        return carry

    lax.fori_loop(0, nk, stage, 0)
    for i in range(nk):
        for j in range(nk):
            gram[i * BLK : (i + 1) * BLK, j * BLK : (j + 1) * BLK] *= down[i] * across[j]
    for t in range(min(nk, 5) + 2, 7):
        csum.step(t)
    gsum.finish()
    csum.finish()


def padded_rows(blocks, unit):
    extra = -blocks.shape[0] % unit
    return jnp.pad(blocks, ((0, extra), (0, 0))) if extra else blocks


def normal_equations(gram_blocks, cross_blocks, k, n_grp, n_shard):
    nk = k // BLK
    unit = 8 * n_grp * n_shard
    gram_blocks = padded_rows(gram_blocks, unit)
    cross_blocks = padded_rows(cross_blocks, unit)
    padded, cross_rows = gram_blocks.shape[0], cross_blocks.shape[0]
    g_parts, g_scratch = sum_scratch(padded, n_grp, n_shard)
    c_parts, c_scratch = sum_scratch(cross_rows, n_grp, n_shard)
    in_vmem = pl.BlockSpec(memory_space=pltpu.VMEM)
    return pl.pallas_call(
        functools.partial(normal_kernel, n_grp, n_shard, nk, g_parts, c_parts),
        out_shape=(
            jax.ShapeDtypeStruct((k, k), jnp.float32),
            jax.ShapeDtypeStruct((cross_rows, BLK), jnp.float32),
        ),
        in_specs=[in_vmem, in_vmem],
        out_specs=(in_vmem, in_vmem),
        scratch_shapes=[
            pltpu.VMEM((padded, BLK), jnp.float32),
            pltpu.VMEM((BLK, k), jnp.float32),
            *g_scratch,
            *c_scratch,
        ],
        compiler_params=pltpu.CompilerParams(
            collective_id=0, has_side_effects=True, vmem_limit_bytes=44 * 2**20
        ),
        name="normal_equations",
    )(gram_blocks, cross_blocks)


def reciprocal(p):
    r = pl.reciprocal(p, approx=True)
    r = r * (2.0 - p * r)
    return r * (2.0 - p * r)


def invert_block(a):
    sub = lax.broadcasted_iota(jnp.int32, (GRP8, BLK), 0)
    lane8 = lax.broadcasted_iota(jnp.int32, (GRP8, BLK), 1)
    lane = lax.broadcasted_iota(jnp.int32, (BLK, BLK), 1)
    for g in range(BLK // GRP8):
        lo = g * GRP8
        cols = [
            jnp.broadcast_to(a[:, lo + c : lo + c + 1], (BLK, BLK)) for c in range(GRP8)
        ]
        own = [c[lo : lo + GRP8, :] for c in cols]
        inside = (lane8 >= lo) & (lane8 < lo + GRP8)
        r = jnp.where(
            inside, jnp.where(lane8 - lo == sub, 1.0, 0.0), a[lo : lo + GRP8, :]
        )
        def spread(t, k):
            return jnp.broadcast_to(t[k : k + 1, :], (GRP8, BLK))

        for k in range(0, GRP8, 2):
            first, second = sub == k, sub == k + 1
            u, v = own[k], own[k + 1]
            p00, p01 = spread(u, k), spread(v, k)
            p10, p11 = spread(u, k + 1), spread(v, k + 1)
            scale = reciprocal(p00 * p11 - p01 * p10)
            m0 = jnp.where(first, -p11, jnp.where(second, p10, u * p11 - v * p10))
            m1 = jnp.where(first, p01, jnp.where(second, -p00, v * p00 - u * p01))
            pivots = first | second

            def eliminate(t):
                change = m0 * spread(t, k) + m1 * spread(t, k + 1)
                return jnp.where(pivots, 0.0, t) - change * scale

            for c in range(k + 2, GRP8):
                own[c] = eliminate(own[c])
            r = eliminate(r)
        rest = jnp.where((lane >= lo) & (lane < lo + GRP8), 0.0, a)
        terms = [
            cols[c] * jnp.broadcast_to(r[c : c + 1, :], (BLK, BLK)) for c in range(GRP8)
        ]
        while len(terms) > 1:
            terms = [terms[i] + terms[i + 1] for i in range(0, len(terms), 2)]
        rest = rest - terms[0]
        pieces = [rest[:lo]] * (lo > 0) + [r] + [rest[lo + GRP8 :]] * (lo + GRP8 < BLK)
        a = jnp.concatenate(pieces, axis=0)
    return a


def solve_kernel(
    nk, nt, tiles, inv_ref, b_ref, x_hbm, y_hbm, pred_ref, res_hbm,
    cross, both, xv, yv, ov, in_sem, out_sem,
):
    load_x = pltpu.make_async_copy(x_hbm, xv, in_sem.at[0])
    load_y = pltpu.make_async_copy(y_hbm, yv, in_sem.at[1])
    load_x.start()
    load_y.start()

    depth = nk * BLK
    for j in range(nt):
        cross[:, j * BLK : (j + 1) * BLK] = b_ref[j * depth : (j + 1) * depth, :]
    pred = dot32(inv_ref[...], cross[...])
    pred_ref[...] = pred
    top = pred.astype(jnp.bfloat16)
    both[:depth, :] = top
    both[depth:, :] = (pred - top.astype(jnp.float32)).astype(jnp.bfloat16)

    load_x.wait()
    load_y.wait()
    rows = xv.shape[0] // tiles
    stores = []
    for t in range(tiles):
        span = pl.ds(t * rows, rows)
        x = xv[span, :]
        estimate = jnp.dot(
            jnp.concatenate([x, x], axis=1), both[...], preferred_element_type=jnp.float32
        )
        ov[span, :] = (yv[span, :].astype(jnp.float32) - estimate).astype(jnp.bfloat16)
        store = pltpu.make_async_copy(ov.at[span, :], res_hbm.at[span, :], out_sem.at[t])
        store.start()
        stores.append(store)
    for store in stores:
        store.wait()


def solve(inverse, total, regressors, targets):
    rows, k = regressors.shape
    p = targets.shape[1]
    tiles = 6 if rows % 96 == 0 else 1
    anywhere = pl.BlockSpec(memory_space=pl.ANY)
    in_vmem = pl.BlockSpec(memory_space=pltpu.VMEM)
    return pl.pallas_call(
        functools.partial(solve_kernel, k // BLK, p // BLK, tiles),
        out_shape=(
            jax.ShapeDtypeStruct((k, p), jnp.float32),
            jax.ShapeDtypeStruct((rows, p), jnp.bfloat16),
        ),
        in_specs=[in_vmem, in_vmem, anywhere, anywhere],
        out_specs=(in_vmem, anywhere),
        scratch_shapes=[
            pltpu.VMEM((k, p), jnp.float32),
            pltpu.VMEM((2 * k, p), jnp.bfloat16),
            pltpu.VMEM((rows, k), jnp.bfloat16),
            pltpu.VMEM((rows, p), jnp.bfloat16),
            pltpu.VMEM((rows, p), jnp.bfloat16),
            pltpu.SemaphoreType.DMA((2,)),
            pltpu.SemaphoreType.DMA((tiles,)),
        ],
        compiler_params=pltpu.CompilerParams(vmem_limit_bytes=48 * 2**20),
        name="solve_and_residual",
    )(inverse, total, regressors, targets)


def body(n_grp, n_shard, regressors, targets):
    contract = (((0,), (0,)), ((), ()))
    gram = lax.dot_general(
        regressors, regressors, contract, preferred_element_type=jnp.float32
    )
    cross = lax.dot_general(
        regressors, targets, contract, preferred_element_type=jnp.float32
    )
    k = gram.shape[0]
    nk, nt = k // BLK, cross.shape[1] // BLK

    def block(i, j):
        return gram[i * BLK : (i + 1) * BLK, j * BLK : (j + 1) * BLK]

    gram_blocks = jnp.concatenate(
        [block(i, j) for i in range(nk) for j in range(i + 1)], axis=0
    )
    cross_blocks = jnp.concatenate(
        [cross[:, j * BLK : (j + 1) * BLK] for j in range(nt)], axis=0
    )
    inverse, total = normal_equations(gram_blocks, cross_blocks, k, n_grp, n_shard)
    return solve(inverse, total, regressors, targets)


def solution(mesh):
    placed = (P(("grp", "shard"), None), P(("grp", "shard"), None))
    return jax.shard_map(
        functools.partial(body, mesh.shape["grp"], mesh.shape["shard"]),
        mesh=mesh,
        in_specs=placed,
        out_specs=(P(), P(("grp", "shard"), None)),
        check_vma=False,
    )
```

```python
import functools

import jax
import jax.numpy as jnp
from jax import lax
from jax.experimental import pallas as pl
from jax.experimental.pallas import tpu as pltpu
from jax.sharding import PartitionSpec as P

MESH = pl.DeviceIdType.MESH
BLK = 128
GRP8 = 8
HIGHEST = lax.Precision.HIGHEST


def dot32(a, b):
    return jnp.dot(a, b, preferred_element_type=jnp.float32, precision=HIGHEST)


def phases(n_grp, n_shard):
    g, s = lax.axis_index("grp"), lax.axis_index("shard")
    cores = 2 if n_grp % 2 == 0 else 1
    ny = n_grp // cores
    nx = ny if n_shard % ny == 0 else 1
    nz = n_shard // nx
    y, core = g // cores, g % cores
    z, x = s // nx, s % nx
    core_ph = (cores, core, lambda q: (y * cores + q, s))
    plane_ph = (
        ny * nx,
        y * nx + x,
        lambda q: ((q // nx) * cores + core, z * nx + q % nx),
    )
    line_ph = (nz, z, lambda q: (g, q * nx + x))
    return core_ph, plane_ph, line_ph


def split_rows(rows, n):
    unit = 8 * n
    units = rows // unit
    if units < 2:
        return (rows,)
    first = max(1, (units * 2 + 1) // 3)
    return (first * unit, (units - first) * unit)


def phase_sizes(n_grp, n_shard, n_parts):
    cores = 2 if n_grp % 2 == 0 else 1
    ny = n_grp // cores
    nx = ny if n_shard % ny == 0 else 1
    nz = n_shard // nx
    return [(cores, ny * nx, nz), (cores, nz, ny * nx)][:n_parts]


class Sum:
    def __init__(self, src, out, parts, orders, scratch):
        self.src, self.out, self.orders = src, out, orders
        self.recv = [scratch[3 * p : 3 * p + 3] for p in range(len(parts))]
        self.acc, *self.sems = scratch[3 * len(parts) :]
        starts = [sum(parts[:p]) for p in range(len(parts))]
        self.bases, self.lens = [], []
        for start, rows, order in zip(starts, parts, orders):
            bases, lens = [start], [rows]
            for m, me, _ in order:
                lens.append(lens[-1] // m)
                bases.append(pl.multiple_of(bases[-1] + me * lens[-1], 8))
            self.bases.append(bases)
            self.lens.append(lens)
        self.n_parts = len(parts)

    def scatter(self, p, i):
        m, me, dev = self.orders[p][i]
        size = self.lens[p][i + 1]
        src = self.src if i == 0 else self.acc
        copies = []
        for d in range(1, m):
            q = (me + d) % m
            at = pl.multiple_of(self.bases[p][i] + q * size, 8)
            copies.append(
                pltpu.make_async_remote_copy(
                    src_ref=src.at[pl.ds(at, size)],
                    dst_ref=self.recv[p][i].at[d - 1],
                    send_sem=self.sems[0].at[p, i, d - 1],
                    recv_sem=self.sems[1].at[p, i, d - 1],
                    device_id=dev(q),
                    device_id_type=MESH,
                )
            )
        return copies

    def gather(self, p, i):
        m, me, dev = self.orders[p][i]
        mine = self.out.at[pl.ds(self.bases[p][i + 1], self.lens[p][i + 1])]
        return [
            pltpu.make_async_remote_copy(
                src_ref=mine,
                dst_ref=mine,
                send_sem=self.sems[2].at[p, i, d - 1],
                recv_sem=self.sems[3].at[p, i, d - 1],
                device_id=dev((me + d) % m),
                device_id_type=MESH,
            )
            for d in range(1, m)
        ]

    def add(self, p, i):
        copies = self.scatter(p, i)
        src = self.src if i == 0 else self.acc
        dst = self.out if i == 2 else self.acc
        span = pl.ds(self.bases[p][i + 1], self.lens[p][i + 1])
        total = src[span]
        for d, copy in enumerate(copies):
            copy.wait_recv()
            total = total + self.recv[p][i][d]
        dst[span] = total

    def step(self, t):
        for p in range(self.n_parts):
            if 1 <= t <= 3:
                self.add(p, t - 1)
            elif t > 3:
                for copy in self.gather(p, 6 - t):
                    copy.wait_recv()
            if t < 3:
                started = self.scatter(p, t)
            elif t < 6:
                started = self.gather(p, 5 - t)
            else:
                started = []
            for copy in started:
                copy.start()

    def finish(self):
        for p in range(self.n_parts):
            for i in range(3):
                for copy in self.scatter(p, i) + self.gather(p, i):
                    copy.wait_send()


def sum_scratch(rows, n_grp, n_shard):
    parts = split_rows(rows, n_grp * n_shard)
    sizes = phase_sizes(n_grp, n_shard, len(parts))
    most = max(max(m) for m in sizes)
    scratch = []
    for part, ms in zip(parts, sizes):
        size = part
        for m in ms:
            size //= m
            scratch.append(pltpu.VMEM((max(m - 1, 1), size, BLK), jnp.float32))
    sems = pltpu.SemaphoreType.DMA((len(parts), 3, max(most - 1, 1)))
    scratch += [pltpu.VMEM((rows, BLK), jnp.float32), sems, sems, sems, sems]
    return parts, scratch


def normal_kernel(
    n_grp, n_shard, nk, g_parts, c_parts, gram_in, cross_in,
    gram, cross_out, gram_out, panel, *scratch,
):
    a, b, c = phases(n_grp, n_shard)
    barrier = pltpu.get_barrier_semaphore()
    count = 0
    for m, me, dev in (a, b, c):
        for d in range(1, m):
            pl.semaphore_signal(
                barrier, inc=1, device_id=dev((me + d) % m), device_id_type=MESH
            )
            count += 1
    pl.semaphore_wait(barrier, count)

    orders = [(a, b, c), (a, c, b)]
    n_first = 3 * len(g_parts) + 5
    gsum = Sum(gram_in, gram_out, g_parts, orders[: len(g_parts)], scratch[:n_first])
    csum = Sum(cross_in, cross_out, c_parts, orders[: len(c_parts)], scratch[n_first:])

    gsum.step(0)
    csum.step(0)
    gsum.step(1)
    gsum.step(2)
    csum.step(1)
    for t in (3, 4, 5, 6):
        gsum.step(t)
    csum.step(2)

    eye = lax.broadcasted_iota(jnp.int32, (BLK, BLK), 0) == lax.broadcasted_iota(
        jnp.int32, (BLK, BLK), 1
    )
    down, across = [], []
    for i in range(nk):
        at = i * (i + 1) // 2 + i
        diagonal = jnp.where(eye, gram_out[at * BLK : (at + 1) * BLK, :], 0.0)
        down.append(lax.rsqrt(jnp.sum(diagonal, axis=1, keepdims=True)))
        across.append(lax.rsqrt(jnp.sum(diagonal, axis=0, keepdims=True)))
    for i in range(nk):
        for j in range(i + 1):
            at = i * (i + 1) // 2 + j
            block = gram_out[at * BLK : (at + 1) * BLK, :] * down[i] * across[j]
            gram[i * BLK : (i + 1) * BLK, j * BLK : (j + 1) * BLK] = block
            if i != j:
                gram[j * BLK : (j + 1) * BLK, i * BLK : (i + 1) * BLK] = block.T

    def stage(j, carry):
        here = pl.ds(pl.multiple_of(j * BLK, BLK), BLK)
        inverse = invert_block(gram[here, here])
        for t in range(min(nk, 4)):
            @pl.when(j == t)
            def _(t=t):
                csum.step(t + 3)

        panel[...] = dot32(inverse, gram[here, :])
        panel[:, here] = inverse
        side = gram[:, here]
        gram[:, here] = jnp.zeros_like(side)
        gram[...] -= dot32(side, panel[...])
        gram[here, :] = panel[...]
        return carry

    lax.fori_loop(0, nk, stage, 0)
    for i in range(nk):
        for j in range(nk):
            gram[i * BLK : (i + 1) * BLK, j * BLK : (j + 1) * BLK] *= down[i] * across[j]
    for t in range(min(nk, 4) + 3, 7):
        csum.step(t)
    gsum.finish()
    csum.finish()


def padded_rows(blocks, unit):
    extra = -blocks.shape[0] % unit
    return jnp.pad(blocks, ((0, extra), (0, 0))) if extra else blocks


def normal_equations(gram_blocks, cross_blocks, k, n_grp, n_shard):
    nk = k // BLK
    unit = 8 * n_grp * n_shard
    gram_blocks = padded_rows(gram_blocks, unit)
    cross_blocks = padded_rows(cross_blocks, unit)
    padded, cross_rows = gram_blocks.shape[0], cross_blocks.shape[0]
    g_parts, g_scratch = sum_scratch(padded, n_grp, n_shard)
    c_parts, c_scratch = sum_scratch(cross_rows, n_grp, n_shard)
    in_vmem = pl.BlockSpec(memory_space=pltpu.VMEM)
    return pl.pallas_call(
        functools.partial(normal_kernel, n_grp, n_shard, nk, g_parts, c_parts),
        out_shape=(
            jax.ShapeDtypeStruct((k, k), jnp.float32),
            jax.ShapeDtypeStruct((cross_rows, BLK), jnp.float32),
        ),
        in_specs=[in_vmem, in_vmem],
        out_specs=(in_vmem, in_vmem),
        scratch_shapes=[
            pltpu.VMEM((padded, BLK), jnp.float32),
            pltpu.VMEM((BLK, k), jnp.float32),
            *g_scratch,
            *c_scratch,
        ],
        compiler_params=pltpu.CompilerParams(
            collective_id=0, has_side_effects=True, vmem_limit_bytes=44 * 2**20
        ),
        name="normal_equations",
    )(gram_blocks, cross_blocks)


def reciprocal(p):
    r = pl.reciprocal(p, approx=True)
    r = r * (2.0 - p * r)
    return r * (2.0 - p * r)


def invert_block(a):
    sub = lax.broadcasted_iota(jnp.int32, (GRP8, BLK), 0)
    lane8 = lax.broadcasted_iota(jnp.int32, (GRP8, BLK), 1)
    lane = lax.broadcasted_iota(jnp.int32, (BLK, BLK), 1)
    for g in range(BLK // GRP8):
        lo = g * GRP8
        cols = [
            jnp.broadcast_to(a[:, lo + c : lo + c + 1], (BLK, BLK)) for c in range(GRP8)
        ]
        own = [c[lo : lo + GRP8, :] for c in cols]
        inside = (lane8 >= lo) & (lane8 < lo + GRP8)
        r = jnp.where(
            inside, jnp.where(lane8 - lo == sub, 1.0, 0.0), a[lo : lo + GRP8, :]
        )
        def spread(t, k):
            return jnp.broadcast_to(t[k : k + 1, :], (GRP8, BLK))

        for k in range(0, GRP8, 2):
            first, second = sub == k, sub == k + 1
            u, v = own[k], own[k + 1]
            p00, p01 = spread(u, k), spread(v, k)
            p10, p11 = spread(u, k + 1), spread(v, k + 1)
            scale = reciprocal(p00 * p11 - p01 * p10)
            m0 = jnp.where(first, -p11, jnp.where(second, p10, u * p11 - v * p10))
            m1 = jnp.where(first, p01, jnp.where(second, -p00, v * p00 - u * p01))
            pivots = first | second

            def eliminate(t):
                change = m0 * spread(t, k) + m1 * spread(t, k + 1)
                return jnp.where(pivots, 0.0, t) - change * scale

            for c in range(k + 2, GRP8):
                own[c] = eliminate(own[c])
            r = eliminate(r)
        rest = jnp.where((lane >= lo) & (lane < lo + GRP8), 0.0, a)
        terms = [
            cols[c] * jnp.broadcast_to(r[c : c + 1, :], (BLK, BLK)) for c in range(GRP8)
        ]
        while len(terms) > 1:
            terms = [terms[i] + terms[i + 1] for i in range(0, len(terms), 2)]
        rest = rest - terms[0]
        pieces = [rest[:lo]] * (lo > 0) + [r] + [rest[lo + GRP8 :]] * (lo + GRP8 < BLK)
        a = jnp.concatenate(pieces, axis=0)
    return a


def solve_kernel(
    nk, nt, tiles, inv_ref, b_ref, x_hbm, y_hbm, pred_ref, res_hbm,
    cross, both, xv, yv, ov, in_sem, out_sem,
):
    load_x = pltpu.make_async_copy(x_hbm, xv, in_sem.at[0])
    load_y = pltpu.make_async_copy(y_hbm, yv, in_sem.at[1])
    load_x.start()
    load_y.start()

    depth = nk * BLK
    for j in range(nt):
        cross[:, j * BLK : (j + 1) * BLK] = b_ref[j * depth : (j + 1) * depth, :]
    pred = dot32(inv_ref[...], cross[...])
    pred_ref[...] = pred
    top = pred.astype(jnp.bfloat16)
    both[:depth, :] = top
    both[depth:, :] = (pred - top.astype(jnp.float32)).astype(jnp.bfloat16)

    load_x.wait()
    load_y.wait()
    rows = xv.shape[0] // tiles
    stores = []
    for t in range(tiles):
        span = pl.ds(t * rows, rows)
        x = xv[span, :]
        estimate = jnp.dot(
            jnp.concatenate([x, x], axis=1), both[...], preferred_element_type=jnp.float32
        )
        ov[span, :] = (yv[span, :].astype(jnp.float32) - estimate).astype(jnp.bfloat16)
        store = pltpu.make_async_copy(ov.at[span, :], res_hbm.at[span, :], out_sem.at[t])
        store.start()
        stores.append(store)
    for store in stores:
        store.wait()


def solve(inverse, total, regressors, targets):
    rows, k = regressors.shape
    p = targets.shape[1]
    tiles = 6 if rows % 96 == 0 else 1
    anywhere = pl.BlockSpec(memory_space=pl.ANY)
    in_vmem = pl.BlockSpec(memory_space=pltpu.VMEM)
    return pl.pallas_call(
        functools.partial(solve_kernel, k // BLK, p // BLK, tiles),
        out_shape=(
            jax.ShapeDtypeStruct((k, p), jnp.float32),
            jax.ShapeDtypeStruct((rows, p), jnp.bfloat16),
        ),
        in_specs=[in_vmem, in_vmem, anywhere, anywhere],
        out_specs=(in_vmem, anywhere),
        scratch_shapes=[
            pltpu.VMEM((k, p), jnp.float32),
            pltpu.VMEM((2 * k, p), jnp.bfloat16),
            pltpu.VMEM((rows, k), jnp.bfloat16),
            pltpu.VMEM((rows, p), jnp.bfloat16),
            pltpu.VMEM((rows, p), jnp.bfloat16),
            pltpu.SemaphoreType.DMA((2,)),
            pltpu.SemaphoreType.DMA((tiles,)),
        ],
        compiler_params=pltpu.CompilerParams(vmem_limit_bytes=48 * 2**20),
        name="solve_and_residual",
    )(inverse, total, regressors, targets)


def body(n_grp, n_shard, regressors, targets):
    contract = (((0,), (0,)), ((), ()))
    gram = lax.dot_general(
        regressors, regressors, contract, preferred_element_type=jnp.float32
    )
    cross = lax.dot_general(
        regressors, targets, contract, preferred_element_type=jnp.float32
    )
    k = gram.shape[0]
    nk, nt = k // BLK, cross.shape[1] // BLK

    def block(i, j):
        return gram[i * BLK : (i + 1) * BLK, j * BLK : (j + 1) * BLK]

    gram_blocks = jnp.concatenate(
        [block(i, j) for i in range(nk) for j in range(i + 1)], axis=0
    )
    cross_blocks = jnp.concatenate(
        [cross[:, j * BLK : (j + 1) * BLK] for j in range(nt)], axis=0
    )
    inverse, total = normal_equations(gram_blocks, cross_blocks, k, n_grp, n_shard)
    return solve(inverse, total, regressors, targets)


def solution(mesh):
    placed = (P(("grp", "shard"), None), P(("grp", "shard"), None))
    return jax.shard_map(
        functools.partial(body, mesh.shape["grp"], mesh.shape["shard"]),
        mesh=mesh,
        in_specs=placed,
        out_specs=(P(), P(("grp", "shard"), None)),
        check_vma=False,
    )
```

```python
import functools

import jax
import jax.numpy as jnp
from jax import lax
from jax.experimental import pallas as pl
from jax.experimental.pallas import tpu as pltpu
from jax.sharding import PartitionSpec as P

MESH = pl.DeviceIdType.MESH
BLK = 128
GRP8 = 8
HIGHEST = lax.Precision.HIGHEST


def dot32(a, b):
    return jnp.dot(a, b, preferred_element_type=jnp.float32, precision=HIGHEST)


def phases(n_grp, n_shard):
    g, s = lax.axis_index("grp"), lax.axis_index("shard")
    cores = 2 if n_grp % 2 == 0 else 1
    ny = n_grp // cores
    nx = ny if n_shard % ny == 0 else 1
    nz = n_shard // nx
    y, core = g // cores, g % cores
    z, x = s // nx, s % nx
    core_ph = (cores, core, lambda q: (y * cores + q, s))
    plane_ph = (
        ny * nx,
        y * nx + x,
        lambda q: ((q // nx) * cores + core, z * nx + q % nx),
    )
    line_ph = (nz, z, lambda q: (g, q * nx + x))
    return core_ph, plane_ph, line_ph


def split_rows(rows, n):
    unit = 8 * n
    units = rows // unit
    if units < 2:
        return (rows,)
    first = max(1, (units * 2 + 1) // 3)
    return (first * unit, (units - first) * unit)


def phase_sizes(n_grp, n_shard, n_parts):
    cores = 2 if n_grp % 2 == 0 else 1
    ny = n_grp // cores
    nx = ny if n_shard % ny == 0 else 1
    nz = n_shard // nx
    return [(cores, ny * nx, nz), (cores, nz, ny * nx)][:n_parts]


class Sum:
    def __init__(self, src, out, parts, orders, scratch):
        self.src, self.out, self.orders = src, out, orders
        self.recv = [scratch[3 * p : 3 * p + 3] for p in range(len(parts))]
        self.acc, *self.sems = scratch[3 * len(parts) :]
        starts = [sum(parts[:p]) for p in range(len(parts))]
        self.bases, self.lens = [], []
        for start, rows, order in zip(starts, parts, orders):
            bases, lens = [start], [rows]
            for m, me, _ in order:
                lens.append(lens[-1] // m)
                bases.append(pl.multiple_of(bases[-1] + me * lens[-1], 8))
            self.bases.append(bases)
            self.lens.append(lens)
        self.n_parts = len(parts)

    def scatter(self, p, i):
        m, me, dev = self.orders[p][i]
        size = self.lens[p][i + 1]
        src = self.src if i == 0 else self.acc
        copies = []
        for d in range(1, m):
            q = (me + d) % m
            at = pl.multiple_of(self.bases[p][i] + q * size, 8)
            copies.append(
                pltpu.make_async_remote_copy(
                    src_ref=src.at[pl.ds(at, size)],
                    dst_ref=self.recv[p][i].at[d - 1],
                    send_sem=self.sems[0].at[p, i, d - 1],
                    recv_sem=self.sems[1].at[p, i, d - 1],
                    device_id=dev(q),
                    device_id_type=MESH,
                )
            )
        return copies

    def gather(self, p, i):
        m, me, dev = self.orders[p][i]
        mine = self.out.at[pl.ds(self.bases[p][i + 1], self.lens[p][i + 1])]
        return [
            pltpu.make_async_remote_copy(
                src_ref=mine,
                dst_ref=mine,
                send_sem=self.sems[2].at[p, i, d - 1],
                recv_sem=self.sems[3].at[p, i, d - 1],
                device_id=dev((me + d) % m),
                device_id_type=MESH,
            )
            for d in range(1, m)
        ]

    def add(self, p, i):
        copies = self.scatter(p, i)
        src = self.src if i == 0 else self.acc
        dst = self.out if i == 2 else self.acc
        span = pl.ds(self.bases[p][i + 1], self.lens[p][i + 1])
        total = src[span]
        for d, copy in enumerate(copies):
            copy.wait_recv()
            total = total + self.recv[p][i][d]
        dst[span] = total

    def step(self, t):
        for p in range(self.n_parts):
            if 1 <= t <= 3:
                self.add(p, t - 1)
            elif t > 3:
                for copy in self.gather(p, 6 - t):
                    copy.wait_recv()
            if t < 3:
                started = self.scatter(p, t)
            elif t < 6:
                started = self.gather(p, 5 - t)
            else:
                started = []
            for copy in started:
                copy.start()

    def finish(self):
        for p in range(self.n_parts):
            for i in range(3):
                for copy in self.scatter(p, i) + self.gather(p, i):
                    copy.wait_send()


def sum_scratch(rows, n_grp, n_shard):
    parts = split_rows(rows, n_grp * n_shard)
    sizes = phase_sizes(n_grp, n_shard, len(parts))
    most = max(max(m) for m in sizes)
    scratch = []
    for part, ms in zip(parts, sizes):
        size = part
        for m in ms:
            size //= m
            scratch.append(pltpu.VMEM((max(m - 1, 1), size, BLK), jnp.float32))
    sems = pltpu.SemaphoreType.DMA((len(parts), 3, max(most - 1, 1)))
    scratch += [pltpu.VMEM((rows, BLK), jnp.float32), sems, sems, sems, sems]
    return parts, scratch


def invert_gram(nk, gram, panel, side, after):
    panel[...] = jnp.zeros_like(panel)
    side[...] = jnp.zeros_like(side)

    def update(i):
        rows = slice(i * BLK, (i + 1) * BLK)
        gram[rows, :] -= dot32(side[rows, :], panel[...])

    updates = [functools.partial(update, i) for i in range(nk)]

    def stage(j, diagonal):
        here = pl.ds(pl.multiple_of(j * BLK, BLK), BLK)
        following = pl.ds(pl.multiple_of(jnp.minimum(j + 1, nk - 1) * BLK, BLK), BLK)
        inverse = invert_block(diagonal, updates)
        panel[...] = dot32(inverse, gram[here, :])
        panel[:, here] = inverse
        side[...] = gram[:, here]
        side[here, :] = jnp.zeros_like(inverse)
        gram[:, here] = jnp.zeros(side.shape, jnp.float32)
        gram[here, :] = panel[...]
        diagonal = gram[following, following] - dot32(
            side[following, :], panel[:, following]
        )
        after(j)
        return diagonal

    lax.fori_loop(0, nk, stage, gram[0:BLK, 0:BLK])
    for work in updates:
        work()


def normal_kernel(
    n_grp, n_shard, nk, g_parts, c_parts, gram_in, cross_in,
    gram, cross_out, gram_out, panel, side, *scratch,
):
    a, b, c = phases(n_grp, n_shard)
    barrier = pltpu.get_barrier_semaphore()
    count = 0
    for m, me, dev in (a, b, c):
        for d in range(1, m):
            pl.semaphore_signal(
                barrier, inc=1, device_id=dev((me + d) % m), device_id_type=MESH
            )
            count += 1
    pl.semaphore_wait(barrier, count)

    orders = [(a, b, c), (a, c, b)]
    n_first = 3 * len(g_parts) + 5
    gsum = Sum(gram_in, gram_out, g_parts, orders[: len(g_parts)], scratch[:n_first])
    csum = Sum(cross_in, cross_out, c_parts, orders[: len(c_parts)], scratch[n_first:])

    gsum.step(0)
    csum.step(0)
    gsum.step(1)
    gsum.step(2)
    csum.step(1)
    for t in (3, 4, 5, 6):
        gsum.step(t)
    csum.step(2)

    eye = lax.broadcasted_iota(jnp.int32, (BLK, BLK), 0) == lax.broadcasted_iota(
        jnp.int32, (BLK, BLK), 1
    )
    down, across = [], []
    for i in range(nk):
        at = i * (i + 1) // 2 + i
        diagonal = jnp.where(eye, gram_out[at * BLK : (at + 1) * BLK, :], 0.0)
        down.append(lax.rsqrt(jnp.sum(diagonal, axis=1, keepdims=True)))
        across.append(lax.rsqrt(jnp.sum(diagonal, axis=0, keepdims=True)))
    for i in range(nk):
        for j in range(i + 1):
            at = i * (i + 1) // 2 + j
            block = gram_out[at * BLK : (at + 1) * BLK, :] * down[i] * across[j]
            gram[i * BLK : (i + 1) * BLK, j * BLK : (j + 1) * BLK] = block
            if i != j:
                gram[j * BLK : (j + 1) * BLK, i * BLK : (i + 1) * BLK] = block.T

    def after(j):
        for t in range(min(nk, 4)):
            @pl.when(j == t)
            def _(t=t):
                csum.step(t + 3)

    invert_gram(nk, gram, panel, side, after)
    for i in range(nk):
        for j in range(nk):
            gram[i * BLK : (i + 1) * BLK, j * BLK : (j + 1) * BLK] *= down[i] * across[j]
    for t in range(min(nk, 4) + 3, 7):
        csum.step(t)
    gsum.finish()
    csum.finish()


def padded_rows(blocks, unit):
    extra = -blocks.shape[0] % unit
    return jnp.pad(blocks, ((0, extra), (0, 0))) if extra else blocks


def normal_equations(gram_blocks, cross_blocks, k, n_grp, n_shard):
    nk = k // BLK
    unit = 8 * n_grp * n_shard
    gram_blocks = padded_rows(gram_blocks, unit)
    cross_blocks = padded_rows(cross_blocks, unit)
    padded, cross_rows = gram_blocks.shape[0], cross_blocks.shape[0]
    g_parts, g_scratch = sum_scratch(padded, n_grp, n_shard)
    c_parts, c_scratch = sum_scratch(cross_rows, n_grp, n_shard)
    in_vmem = pl.BlockSpec(memory_space=pltpu.VMEM)
    return pl.pallas_call(
        functools.partial(normal_kernel, n_grp, n_shard, nk, g_parts, c_parts),
        out_shape=(
            jax.ShapeDtypeStruct((k, k), jnp.float32),
            jax.ShapeDtypeStruct((cross_rows, BLK), jnp.float32),
        ),
        in_specs=[in_vmem, in_vmem],
        out_specs=(in_vmem, in_vmem),
        scratch_shapes=[
            pltpu.VMEM((padded, BLK), jnp.float32),
            pltpu.VMEM((BLK, k), jnp.float32),
            pltpu.VMEM((k, BLK), jnp.float32),
            *g_scratch,
            *c_scratch,
        ],
        compiler_params=pltpu.CompilerParams(
            collective_id=0, has_side_effects=True, vmem_limit_bytes=44 * 2**20
        ),
        name="normal_equations",
    )(gram_blocks, cross_blocks)


def reciprocal(p):
    r = pl.reciprocal(p, approx=True)
    r = r * (2.0 - p * r)
    return r * (2.0 - p * r)


def invert_block(a, beside=()):
    sub = lax.broadcasted_iota(jnp.int32, (GRP8, BLK), 0)
    lane8 = lax.broadcasted_iota(jnp.int32, (GRP8, BLK), 1)
    lane = lax.broadcasted_iota(jnp.int32, (BLK, BLK), 1)
    for g in range(BLK // GRP8):
        lo = g * GRP8
        for t, work in enumerate(beside):
            if t * (BLK // GRP8) // len(beside) == g:
                work()
        cols = [
            jnp.broadcast_to(a[:, lo + c : lo + c + 1], (BLK, BLK)) for c in range(GRP8)
        ]
        own = [c[lo : lo + GRP8, :] for c in cols]
        inside = (lane8 >= lo) & (lane8 < lo + GRP8)
        r = jnp.where(
            inside, jnp.where(lane8 - lo == sub, 1.0, 0.0), a[lo : lo + GRP8, :]
        )
        def spread(t, k):
            return jnp.broadcast_to(t[k : k + 1, :], (GRP8, BLK))

        for k in range(0, GRP8, 2):
            first, second = sub == k, sub == k + 1
            u, v = own[k], own[k + 1]
            p00, p01 = spread(u, k), spread(v, k)
            p10, p11 = spread(u, k + 1), spread(v, k + 1)
            scale = reciprocal(p00 * p11 - p01 * p10)
            m0 = jnp.where(first, -p11, jnp.where(second, p10, u * p11 - v * p10))
            m1 = jnp.where(first, p01, jnp.where(second, -p00, v * p00 - u * p01))
            pivots = first | second

            def eliminate(t):
                change = m0 * spread(t, k) + m1 * spread(t, k + 1)
                return jnp.where(pivots, 0.0, t) - change * scale

            for c in range(k + 2, GRP8):
                own[c] = eliminate(own[c])
            r = eliminate(r)
        rest = jnp.where((lane >= lo) & (lane < lo + GRP8), 0.0, a)
        terms = [
            cols[c] * jnp.broadcast_to(r[c : c + 1, :], (BLK, BLK)) for c in range(GRP8)
        ]
        while len(terms) > 1:
            terms = [terms[i] + terms[i + 1] for i in range(0, len(terms), 2)]
        rest = rest - terms[0]
        pieces = [rest[:lo]] * (lo > 0) + [r] + [rest[lo + GRP8 :]] * (lo + GRP8 < BLK)
        a = jnp.concatenate(pieces, axis=0)
    return a


def solve_kernel(
    nk, nt, tiles, inv_ref, b_ref, x_hbm, y_hbm, pred_ref, res_hbm,
    cross, both, xv, yv, ov, in_sem, out_sem,
):
    load_x = pltpu.make_async_copy(x_hbm, xv, in_sem.at[0])
    load_y = pltpu.make_async_copy(y_hbm, yv, in_sem.at[1])
    load_x.start()
    load_y.start()

    depth = nk * BLK
    for j in range(nt):
        cross[:, j * BLK : (j + 1) * BLK] = b_ref[j * depth : (j + 1) * depth, :]
    pred = dot32(inv_ref[...], cross[...])
    pred_ref[...] = pred
    top = pred.astype(jnp.bfloat16)
    both[:depth, :] = top
    both[depth:, :] = (pred - top.astype(jnp.float32)).astype(jnp.bfloat16)

    load_x.wait()
    load_y.wait()
    rows = xv.shape[0] // tiles
    stores = []
    for t in range(tiles):
        span = pl.ds(t * rows, rows)
        x = xv[span, :]
        estimate = jnp.dot(
            jnp.concatenate([x, x], axis=1), both[...], preferred_element_type=jnp.float32
        )
        ov[span, :] = (yv[span, :].astype(jnp.float32) - estimate).astype(jnp.bfloat16)
        store = pltpu.make_async_copy(ov.at[span, :], res_hbm.at[span, :], out_sem.at[t])
        store.start()
        stores.append(store)
    for store in stores:
        store.wait()


def solve(inverse, total, regressors, targets):
    rows, k = regressors.shape
    p = targets.shape[1]
    tiles = 6 if rows % 96 == 0 else 1
    anywhere = pl.BlockSpec(memory_space=pl.ANY)
    in_vmem = pl.BlockSpec(memory_space=pltpu.VMEM)
    return pl.pallas_call(
        functools.partial(solve_kernel, k // BLK, p // BLK, tiles),
        out_shape=(
            jax.ShapeDtypeStruct((k, p), jnp.float32),
            jax.ShapeDtypeStruct((rows, p), jnp.bfloat16),
        ),
        in_specs=[in_vmem, in_vmem, anywhere, anywhere],
        out_specs=(in_vmem, anywhere),
        scratch_shapes=[
            pltpu.VMEM((k, p), jnp.float32),
            pltpu.VMEM((2 * k, p), jnp.bfloat16),
            pltpu.VMEM((rows, k), jnp.bfloat16),
            pltpu.VMEM((rows, p), jnp.bfloat16),
            pltpu.VMEM((rows, p), jnp.bfloat16),
            pltpu.SemaphoreType.DMA((2,)),
            pltpu.SemaphoreType.DMA((tiles,)),
        ],
        compiler_params=pltpu.CompilerParams(vmem_limit_bytes=48 * 2**20),
        name="solve_and_residual",
    )(inverse, total, regressors, targets)


def body(n_grp, n_shard, regressors, targets):
    contract = (((0,), (0,)), ((), ()))
    gram = lax.dot_general(
        regressors, regressors, contract, preferred_element_type=jnp.float32
    )
    cross = lax.dot_general(
        regressors, targets, contract, preferred_element_type=jnp.float32
    )
    k = gram.shape[0]
    nk, nt = k // BLK, cross.shape[1] // BLK

    def block(i, j):
        return gram[i * BLK : (i + 1) * BLK, j * BLK : (j + 1) * BLK]

    gram_blocks = jnp.concatenate(
        [block(i, j) for i in range(nk) for j in range(i + 1)], axis=0
    )
    cross_blocks = jnp.concatenate(
        [cross[:, j * BLK : (j + 1) * BLK] for j in range(nt)], axis=0
    )
    inverse, total = normal_equations(gram_blocks, cross_blocks, k, n_grp, n_shard)
    return solve(inverse, total, regressors, targets)


def solution(mesh):
    placed = (P(("grp", "shard"), None), P(("grp", "shard"), None))
    return jax.shard_map(
        functools.partial(body, mesh.shape["grp"], mesh.shape["shard"]),
        mesh=mesh,
        in_specs=placed,
        out_specs=(P(), P(("grp", "shard"), None)),
        check_vma=False,
    )
```

```python
import functools

import jax
import jax.numpy as jnp
from jax import lax
from jax.experimental import pallas as pl
from jax.experimental.pallas import tpu as pltpu
from jax.sharding import PartitionSpec as P

MESH = pl.DeviceIdType.MESH
BLK = 128
GRP8 = 8
HIGHEST = lax.Precision.HIGHEST


def dot32(a, b):
    return jnp.dot(a, b, preferred_element_type=jnp.float32, precision=HIGHEST)


def phases(n_grp, n_shard):
    g, s = lax.axis_index("grp"), lax.axis_index("shard")
    cores = 2 if n_grp % 2 == 0 else 1
    ny = n_grp // cores
    nx = ny if n_shard % ny == 0 else 1
    nz = n_shard // nx
    y, core = g // cores, g % cores
    z, x = s // nx, s % nx
    core_ph = (cores, core, lambda q: (y * cores + q, s))
    plane_ph = (
        ny * nx,
        y * nx + x,
        lambda q: ((q // nx) * cores + core, z * nx + q % nx),
    )
    line_ph = (nz, z, lambda q: (g, q * nx + x))
    return core_ph, plane_ph, line_ph


def split_rows(rows, n):
    unit = 8 * n
    units = rows // unit
    if units < 2:
        return (rows,)
    first = max(1, (units * 2 + 1) // 3)
    return (first * unit, (units - first) * unit)


def phase_sizes(n_grp, n_shard, n_parts):
    cores = 2 if n_grp % 2 == 0 else 1
    ny = n_grp // cores
    nx = ny if n_shard % ny == 0 else 1
    nz = n_shard // nx
    return [(cores, ny * nx, nz), (cores, nz, ny * nx)][:n_parts]


class Sum:
    def __init__(self, src, out, parts, orders, scratch):
        self.src, self.out, self.orders = src, out, orders
        self.recv = [scratch[3 * p : 3 * p + 3] for p in range(len(parts))]
        self.acc, *self.sems = scratch[3 * len(parts) :]
        starts = [sum(parts[:p]) for p in range(len(parts))]
        self.bases, self.lens = [], []
        for start, rows, order in zip(starts, parts, orders):
            bases, lens = [start], [rows]
            for m, me, _ in order:
                lens.append(lens[-1] // m)
                bases.append(pl.multiple_of(bases[-1] + me * lens[-1], 8))
            self.bases.append(bases)
            self.lens.append(lens)
        self.n_parts = len(parts)

    def scatter(self, p, i):
        m, me, dev = self.orders[p][i]
        size = self.lens[p][i + 1]
        src = self.src if i == 0 else self.acc
        copies = []
        for d in range(1, m):
            q = (me + d) % m
            at = pl.multiple_of(self.bases[p][i] + q * size, 8)
            copies.append(
                pltpu.make_async_remote_copy(
                    src_ref=src.at[pl.ds(at, size)],
                    dst_ref=self.recv[p][i].at[d - 1],
                    send_sem=self.sems[0].at[p, i, d - 1],
                    recv_sem=self.sems[1].at[p, i, d - 1],
                    device_id=dev(q),
                    device_id_type=MESH,
                )
            )
        return copies

    def gather(self, p, i):
        m, me, dev = self.orders[p][i]
        mine = self.out.at[pl.ds(self.bases[p][i + 1], self.lens[p][i + 1])]
        return [
            pltpu.make_async_remote_copy(
                src_ref=mine,
                dst_ref=mine,
                send_sem=self.sems[2].at[p, i, d - 1],
                recv_sem=self.sems[3].at[p, i, d - 1],
                device_id=dev((me + d) % m),
                device_id_type=MESH,
            )
            for d in range(1, m)
        ]

    def add(self, p, i):
        copies = self.scatter(p, i)
        src = self.src if i == 0 else self.acc
        dst = self.out if i == 2 else self.acc
        span = pl.ds(self.bases[p][i + 1], self.lens[p][i + 1])
        total = src[span]
        for d, copy in enumerate(copies):
            copy.wait_recv()
            total = total + self.recv[p][i][d]
        dst[span] = total

    def step(self, t):
        for p in range(self.n_parts):
            if 1 <= t <= 3:
                self.add(p, t - 1)
            elif t > 3:
                for copy in self.gather(p, 6 - t):
                    copy.wait_recv()
            if t < 3:
                started = self.scatter(p, t)
            elif t < 6:
                started = self.gather(p, 5 - t)
            else:
                started = []
            for copy in started:
                copy.start()

    def finish(self):
        for p in range(self.n_parts):
            for i in range(3):
                for copy in self.scatter(p, i) + self.gather(p, i):
                    copy.wait_send()


def sum_scratch(rows, n_grp, n_shard):
    parts = split_rows(rows, n_grp * n_shard)
    sizes = phase_sizes(n_grp, n_shard, len(parts))
    most = max(max(m) for m in sizes)
    scratch = []
    for part, ms in zip(parts, sizes):
        size = part
        for m in ms:
            size //= m
            scratch.append(pltpu.VMEM((max(m - 1, 1), size, BLK), jnp.float32))
    sems = pltpu.SemaphoreType.DMA((len(parts), 3, max(most - 1, 1)))
    scratch += [pltpu.VMEM((rows, BLK), jnp.float32), sems, sems, sems, sems]
    return parts, scratch


def invert_gram(nk, gram, panel, side, after):
    panel[...] = jnp.zeros_like(panel)
    side[...] = jnp.zeros_like(side)

    def update(i):
        rows = slice(i * BLK, (i + 1) * BLK)
        gram[rows, :] -= dot32(side[rows, :], panel[...])

    updates = [functools.partial(update, i) for i in range(nk)]

    def stage(j, diagonal):
        here = pl.ds(pl.multiple_of(j * BLK, BLK), BLK)
        following = pl.ds(pl.multiple_of(jnp.minimum(j + 1, nk - 1) * BLK, BLK), BLK)
        inverse = invert_block(diagonal, updates)
        panel[...] = dot32(inverse, gram[here, :])
        panel[:, here] = inverse
        side[...] = gram[:, here]
        side[here, :] = jnp.zeros_like(inverse)
        gram[:, here] = jnp.zeros(side.shape, jnp.float32)
        gram[here, :] = panel[...]
        diagonal = gram[following, following] - dot32(
            side[following, :], panel[:, following]
        )
        after(j)
        return diagonal

    lax.fori_loop(0, nk, stage, gram[0:BLK, 0:BLK])
    for work in updates:
        work()


def normal_kernel(
    n_grp, n_shard, nk, g_parts, c_parts, gram_in, x_hbm, y_hbm,
    gram, cross_out, xv, yv, cross_in, gram_out, panel, side, in_sem, *scratch,
):
    load_x = pltpu.make_async_copy(x_hbm, xv, in_sem.at[0])
    load_y = pltpu.make_async_copy(y_hbm, yv, in_sem.at[1])
    load_x.start()
    load_y.start()

    a, b, c = phases(n_grp, n_shard)
    barrier = pltpu.get_barrier_semaphore()
    count = 0
    for m, me, dev in (a, b, c):
        for d in range(1, m):
            pl.semaphore_signal(
                barrier, inc=1, device_id=dev((me + d) % m), device_id_type=MESH
            )
            count += 1
    pl.semaphore_wait(barrier, count)

    orders = [(a, b, c), (a, c, b)]
    n_first = 3 * len(g_parts) + 5
    gsum = Sum(gram_in, gram_out, g_parts, orders[: len(g_parts)], scratch[:n_first])
    csum = Sum(cross_in, cross_out, c_parts, orders[: len(c_parts)], scratch[n_first:])

    gsum.step(0)
    load_x.wait()
    load_y.wait()
    frames, k = xv.shape
    used = yv.shape[1] // BLK * k
    if used < cross_in.shape[0]:
        cross_in[used:, :] = jnp.zeros((cross_in.shape[0] - used, BLK), jnp.float32)

    def cross_half(h):
        span = slice(h * (frames // 2), (h + 1) * (frames // 2))
        part = lax.dot_general(
            xv[span, :],
            yv[span, :],
            (((0,), (0,)), ((), ())),
            preferred_element_type=jnp.float32,
        )
        for j in range(used // k):
            piece = part[:, j * BLK : (j + 1) * BLK]
            if h:
                piece = cross_in[j * k : (j + 1) * k, :] + piece
            cross_in[j * k : (j + 1) * k, :] = piece

    gsum.step(1)
    cross_half(0)
    gsum.step(2)
    cross_half(1)
    gsum.step(3)
    csum.step(0)
    gsum.step(4)
    gsum.step(5)
    csum.step(1)
    gsum.step(6)

    eye = lax.broadcasted_iota(jnp.int32, (BLK, BLK), 0) == lax.broadcasted_iota(
        jnp.int32, (BLK, BLK), 1
    )
    down, across = [], []
    for i in range(nk):
        at = i * (i + 1) // 2 + i
        diagonal = jnp.where(eye, gram_out[at * BLK : (at + 1) * BLK, :], 0.0)
        down.append(lax.rsqrt(jnp.sum(diagonal, axis=1, keepdims=True)))
        across.append(lax.rsqrt(jnp.sum(diagonal, axis=0, keepdims=True)))
    for i in range(nk):
        for j in range(i + 1):
            at = i * (i + 1) // 2 + j
            block = gram_out[at * BLK : (at + 1) * BLK, :] * down[i] * across[j]
            gram[i * BLK : (i + 1) * BLK, j * BLK : (j + 1) * BLK] = block
            if i != j:
                gram[j * BLK : (j + 1) * BLK, i * BLK : (i + 1) * BLK] = block.T

    csum.step(2)

    def after(j):
        for t in range(min(nk, 4)):
            @pl.when(j == t)
            def _(t=t):
                csum.step(t + 3)

    invert_gram(nk, gram, panel, side, after)
    for i in range(nk):
        for j in range(nk):
            gram[i * BLK : (i + 1) * BLK, j * BLK : (j + 1) * BLK] *= down[i] * across[j]
    for t in range(min(nk, 4) + 3, 7):
        csum.step(t)
    gsum.finish()
    csum.finish()


def normal_equations(gram_blocks, regressors, targets, n_grp, n_shard):
    frames, k = regressors.shape
    p = targets.shape[1]
    nk = k // BLK
    unit = 8 * n_grp * n_shard
    extra = -gram_blocks.shape[0] % unit
    if extra:
        gram_blocks = jnp.pad(gram_blocks, ((0, extra), (0, 0)))
    padded = gram_blocks.shape[0]
    cross_rows = -(-(p // BLK * k) // unit) * unit
    g_parts, g_scratch = sum_scratch(padded, n_grp, n_shard)
    c_parts, c_scratch = sum_scratch(cross_rows, n_grp, n_shard)
    in_vmem = pl.BlockSpec(memory_space=pltpu.VMEM)
    return pl.pallas_call(
        functools.partial(normal_kernel, n_grp, n_shard, nk, g_parts, c_parts),
        out_shape=(
            jax.ShapeDtypeStruct((k, k), jnp.float32),
            jax.ShapeDtypeStruct((cross_rows, BLK), jnp.float32),
        ),
        in_specs=[in_vmem] + [pl.BlockSpec(memory_space=pl.ANY)] * 2,
        out_specs=(in_vmem, in_vmem),
        scratch_shapes=[
            pltpu.VMEM((frames, k), jnp.bfloat16),
            pltpu.VMEM((frames, p), jnp.bfloat16),
            pltpu.VMEM((cross_rows, BLK), jnp.float32),
            pltpu.VMEM((padded, BLK), jnp.float32),
            pltpu.VMEM((BLK, k), jnp.float32),
            pltpu.VMEM((k, BLK), jnp.float32),
            pltpu.SemaphoreType.DMA((2,)),
            *g_scratch,
            *c_scratch,
        ],
        compiler_params=pltpu.CompilerParams(
            collective_id=0, has_side_effects=True, vmem_limit_bytes=44 * 2**20
        ),
        name="normal_equations",
    )(gram_blocks, regressors, targets)


def reciprocal(p):
    r = pl.reciprocal(p, approx=True)
    r = r * (2.0 - p * r)
    return r * (2.0 - p * r)


def invert_block(a, beside=()):
    sub = lax.broadcasted_iota(jnp.int32, (GRP8, BLK), 0)
    lane8 = lax.broadcasted_iota(jnp.int32, (GRP8, BLK), 1)
    lane = lax.broadcasted_iota(jnp.int32, (BLK, BLK), 1)
    for g in range(BLK // GRP8):
        lo = g * GRP8
        for t, work in enumerate(beside):
            if t * (BLK // GRP8) // len(beside) == g:
                work()
        cols = [
            jnp.broadcast_to(a[:, lo + c : lo + c + 1], (BLK, BLK)) for c in range(GRP8)
        ]
        own = [c[lo : lo + GRP8, :] for c in cols]
        inside = (lane8 >= lo) & (lane8 < lo + GRP8)
        r = jnp.where(
            inside, jnp.where(lane8 - lo == sub, 1.0, 0.0), a[lo : lo + GRP8, :]
        )
        def spread(t, k):
            return jnp.broadcast_to(t[k : k + 1, :], (GRP8, BLK))

        for k in range(0, GRP8, 2):
            first, second = sub == k, sub == k + 1
            u, v = own[k], own[k + 1]
            p00, p01 = spread(u, k), spread(v, k)
            p10, p11 = spread(u, k + 1), spread(v, k + 1)
            scale = reciprocal(p00 * p11 - p01 * p10)
            m0 = jnp.where(first, -p11, jnp.where(second, p10, u * p11 - v * p10))
            m1 = jnp.where(first, p01, jnp.where(second, -p00, v * p00 - u * p01))
            pivots = first | second

            def eliminate(t):
                change = m0 * spread(t, k) + m1 * spread(t, k + 1)
                return jnp.where(pivots, 0.0, t) - change * scale

            for c in range(k + 2, GRP8):
                own[c] = eliminate(own[c])
            r = eliminate(r)
        rest = jnp.where((lane >= lo) & (lane < lo + GRP8), 0.0, a)
        terms = [
            cols[c] * jnp.broadcast_to(r[c : c + 1, :], (BLK, BLK)) for c in range(GRP8)
        ]
        while len(terms) > 1:
            terms = [terms[i] + terms[i + 1] for i in range(0, len(terms), 2)]
        rest = rest - terms[0]
        pieces = [rest[:lo]] * (lo > 0) + [r] + [rest[lo + GRP8 :]] * (lo + GRP8 < BLK)
        a = jnp.concatenate(pieces, axis=0)
    return a


def solve_kernel(
    nk, nt, tiles, inv_ref, b_ref, x_hbm, y_hbm, pred_ref, res_hbm,
    cross, both, xv, yv, ov, in_sem, out_sem,
):
    load_x = pltpu.make_async_copy(x_hbm, xv, in_sem.at[0])
    load_y = pltpu.make_async_copy(y_hbm, yv, in_sem.at[1])
    load_x.start()
    load_y.start()

    depth = nk * BLK
    for j in range(nt):
        cross[:, j * BLK : (j + 1) * BLK] = b_ref[j * depth : (j + 1) * depth, :]
    pred = dot32(inv_ref[...], cross[...])
    pred_ref[...] = pred
    top = pred.astype(jnp.bfloat16)
    both[:depth, :] = top
    both[depth:, :] = (pred - top.astype(jnp.float32)).astype(jnp.bfloat16)

    load_x.wait()
    load_y.wait()
    rows = xv.shape[0] // tiles
    stores = []
    for t in range(tiles):
        span = pl.ds(t * rows, rows)
        x = xv[span, :]
        estimate = jnp.dot(
            jnp.concatenate([x, x], axis=1), both[...], preferred_element_type=jnp.float32
        )
        ov[span, :] = (yv[span, :].astype(jnp.float32) - estimate).astype(jnp.bfloat16)
        store = pltpu.make_async_copy(ov.at[span, :], res_hbm.at[span, :], out_sem.at[t])
        store.start()
        stores.append(store)
    for store in stores:
        store.wait()


def solve(inverse, total, regressors, targets):
    rows, k = regressors.shape
    p = targets.shape[1]
    tiles = 6 if rows % 96 == 0 else 1
    anywhere = pl.BlockSpec(memory_space=pl.ANY)
    in_vmem = pl.BlockSpec(memory_space=pltpu.VMEM)
    return pl.pallas_call(
        functools.partial(solve_kernel, k // BLK, p // BLK, tiles),
        out_shape=(
            jax.ShapeDtypeStruct((k, p), jnp.float32),
            jax.ShapeDtypeStruct((rows, p), jnp.bfloat16),
        ),
        in_specs=[in_vmem, in_vmem, anywhere, anywhere],
        out_specs=(in_vmem, anywhere),
        scratch_shapes=[
            pltpu.VMEM((k, p), jnp.float32),
            pltpu.VMEM((2 * k, p), jnp.bfloat16),
            pltpu.VMEM((rows, k), jnp.bfloat16),
            pltpu.VMEM((rows, p), jnp.bfloat16),
            pltpu.VMEM((rows, p), jnp.bfloat16),
            pltpu.SemaphoreType.DMA((2,)),
            pltpu.SemaphoreType.DMA((tiles,)),
        ],
        compiler_params=pltpu.CompilerParams(vmem_limit_bytes=48 * 2**20),
        name="solve_and_residual",
    )(inverse, total, regressors, targets)


def body(n_grp, n_shard, regressors, targets):
    contract = (((0,), (0,)), ((), ()))
    gram = lax.dot_general(
        regressors, regressors, contract, preferred_element_type=jnp.float32
    )
    nk = gram.shape[0] // BLK

    def block(i, j):
        return gram[i * BLK : (i + 1) * BLK, j * BLK : (j + 1) * BLK]

    gram_blocks = jnp.concatenate(
        [block(i, j) for i in range(nk) for j in range(i + 1)], axis=0
    )
    inverse, total = normal_equations(
        gram_blocks, regressors, targets, n_grp, n_shard
    )
    return solve(inverse, total, regressors, targets)


def solution(mesh):
    placed = (P(("grp", "shard"), None), P(("grp", "shard"), None))
    return jax.shard_map(
        functools.partial(body, mesh.shape["grp"], mesh.shape["shard"]),
        mesh=mesh,
        in_specs=placed,
        out_specs=(P(), P(("grp", "shard"), None)),
        check_vma=False,
    )
```
